128 devices in a mesh: axial: 16 (over y_hi, x, core), seq: 8 (over y_lo, z).
Axes of the slice: x: 4, y: 4 (y_hi: 2, y_lo: 2; y = y_hi * 2 + y_lo), z: 4, core: 2. Of those that a mesh axis runs over, the one named last changes fastest.
Arguments:
- homolog_features: bfloat16 [432, 131072], P('seq', 'axial'), may hold values from -6 to 6
- residue_couple_features: bfloat16 [2048, 2048, 128], P('axial', 'seq')
- residue_validity: int32 [2048], replicated, may hold values from 0 to 1, as said below
- homolog_validity: int32 [432], P('seq'), may hold values 0 or 1
- content_projection_matrix: bfloat16 [64, 64], replicated, may hold values from -0.75 to 0.75
- sigmoid_projection_matrix: bfloat16 [64, 64], replicated, may hold values from -0.75 to 0.75
- logit_projection_matrix: bfloat16 [128, 8], replicated
- final_projection_matrix: bfloat16 [64, 64], replicated, may hold values from -0.75 to 0.75
- result_adjoint: bfloat16 [432, 131072], P('seq', 'axial'), may hold values from -6 to 6
Outputs:
- module_result: bfloat16 [432, 131072], P('seq', 'axial')
- homolog_feature_derivative: bfloat16 [432, 131072], P('seq', 'axial')
- pairwise_gradient: bfloat16 [2048, 2048, 128], P('axial', 'seq')
- value_weight_gradient: float32 [64, 64], replicated
- gate_weight_gradient: float32 [64, 64], replicated
- bias_weight_gradient: float32 [128, 8], replicated
- output_weight_gradient: float32 [64, 64], replicated
The draws below stay inside these ranges and needn't reach their ends.
Inputs may be any that keep to these rules, and one draw needn't show every extreme that they name: `residue_validity`: token 0 is always 1.
All inputs are finite; a program needn't handle non-finite values. No bound on the sum of `homolog_validity` on one device may be relied on, other than what follows from the above.
Results may differ from the reference program's by a relative error of at most 0.023.
The reference program's roundings to bfloat16 on the way count: a program that leaves them out, or rounds other values in their place, can miss the bound.
Values may be sent and summed in bfloat16 or wider, within the bound.
No kernel may reach another device: no remote copies, remote signals or barrier semaphores. Data moves between devices by JAX's collectives and lax.ppermute only.
A program may use at most 192 MiB of HBM per device.

```python
import math
import jax
import jax.numpy as jnp
from jax import lax

FEATURE_WIDTH = 64
CZ = 128
HEADS = 8
HEAD_CH = 8
TOK_DEV = 128
SEQ_DEV = 54
RESIDUE_NUMBER = 2048
HOMOLOG_NUMBER = 432
N_SEQ = 8


def pair_direction(key):
    return jax.random.normal(key, (CZ, HEADS), jnp.float32)


def draw_logit_projection_matrix(key, part):
    base = pair_direction(key)
    factor = 1.5 / math.sqrt(CZ)
    return (base * factor).astype(jnp.bfloat16)


def draw_residue_couple_features(key, part):
    key = jax.random.fold_in(key, 11)
    noise_key = jax.random.fold_in(key, 0)
    noise = jax.random.normal(noise_key, (RESIDUE_NUMBER, RESIDUE_NUMBER, CZ), jnp.float32)
    return noise.astype(jnp.bfloat16)


def draw_residue_validity(key, part):
    key = jax.random.fold_in(key, 5)
    live = (jax.random.randint(key, (RESIDUE_NUMBER,), 0, 8) >= 1).astype(jnp.int32)
    return jnp.where(jnp.arange(RESIDUE_NUMBER) == 0, 1, live).astype(jnp.int32)


def set_ends(result, own_key, least, top_value):
    extent = result.shape
    index_at = [jax.random.randint(jax.random.fold_in(own_key, axis), (), 0, extent[axis]) for axis in range(len(extent))]
    result = result.at[tuple(index_at)].set(least)
    longest = extent.index(max(extent))
    index_at[longest] = (index_at[longest] + 1) % extent[longest]
    return result.at[tuple(index_at)].set(top_value)


def levels(stream_key, extent, cuts, smallest, largest):
    level, own = 1.0, jax.random.fold_in(stream_key, 6)
    for position, shards_of in cuts:
        heights = jnp.exp(jax.random.uniform(jax.random.fold_in(own, position), (shards_of,), jnp.float32, smallest / len(cuts), largest / len(cuts)))
        level = level * jnp.repeat(heights, extent[position] // shards_of).reshape([-1 if axis == position else 1 for axis in range(len(extent))])
    return level


def scatter_about(key, extent, width, reach, cuts=(), dtype=jnp.bfloat16):
    entries = jax.random.normal(key, extent, jnp.float32) * width
    if len(cuts) > 0:
        entries = levels(key, extent, cuts, -0.22, 0.18) * entries
    return jnp.clip(entries, min=-reach, max=reach).astype(dtype)


def setup_inputs(seed: int = 0) -> dict:
    key_list = jax.random.split(jax.random.key(seed), 10)
    homolog_features = scatter_about(key_list[0], (HOMOLOG_NUMBER, RESIDUE_NUMBER * FEATURE_WIDTH), 1.0, 6.0, ((0, 8), (1, 16)))
    residue_couple_features = draw_residue_couple_features(jax.random.fold_in(key_list[9], 71), 0)
    residue_validity = draw_residue_validity(jax.random.fold_in(key_list[9], 71), 0)
    homolog_validity = set_ends((jax.random.randint(key_list[3], (HOMOLOG_NUMBER,), 0, 8) < 7).astype(jnp.int32), jax.random.fold_in(key_list[3], 1), 0, 1)
    content_projection_matrix = scatter_about(key_list[4], (FEATURE_WIDTH, FEATURE_WIDTH), FEATURE_WIDTH ** -0.5, 0.75)
    sigmoid_projection_matrix = scatter_about(key_list[5], (FEATURE_WIDTH, FEATURE_WIDTH), FEATURE_WIDTH ** -0.5, 0.75)
    logit_projection_matrix = draw_logit_projection_matrix(jax.random.fold_in(key_list[9], 71), 0)
    final_projection_matrix = scatter_about(key_list[7], (FEATURE_WIDTH, FEATURE_WIDTH), FEATURE_WIDTH ** -0.5, 0.75)
    result_adjoint = scatter_about(key_list[8], (HOMOLOG_NUMBER, RESIDUE_NUMBER * FEATURE_WIDTH), 1.0, 6.0, ((0, 8), (1, 16)))
    return {"homolog_features": homolog_features, "residue_couple_features": residue_couple_features, "residue_validity": residue_validity, "homolog_validity": homolog_validity, "content_projection_matrix": content_projection_matrix, "sigmoid_projection_matrix": sigmoid_projection_matrix, "logit_projection_matrix": logit_projection_matrix, "final_projection_matrix": final_projection_matrix, "result_adjoint": result_adjoint}


def standardize_features(inputs):
    center = inputs - lax.optimization_barrier(jnp.mean(inputs, axis=-1, keepdims=True))
    scale = lax.rsqrt(lax.optimization_barrier(jnp.mean(center * center, axis=-1, keepdims=True)) + 1e-05)
    return (center * scale, scale)

def standardize_backward(incoming_adjoint, normed, scale):
    first = lax.optimization_barrier(jnp.mean(incoming_adjoint, axis=-1, keepdims=True))
    second = lax.optimization_barrier(jnp.mean(incoming_adjoint * normed, axis=-1, keepdims=True))
    return scale * (incoming_adjoint - first - normed * second)

def reference(homolog_features, residue_couple_features, residue_validity, homolog_validity, content_projection_matrix, sigmoid_projection_matrix, logit_projection_matrix, final_projection_matrix, result_adjoint):
    homolog_entries = homolog_features.shape[0]
    residue_tally = residue_couple_features.shape[0]
    blocks = residue_tally // TOK_DEV
    homolog_standardized, homolog_standardize_factor = standardize_features(homolog_features.reshape(homolog_entries, residue_tally, FEATURE_WIDTH).astype(jnp.float32))
    standardized_halfwidth = homolog_standardized.astype(jnp.bfloat16).reshape(-1, FEATURE_WIDTH)
    projected_entries = jnp.dot(standardized_halfwidth, content_projection_matrix, preferred_element_type=jnp.float32).astype(jnp.bfloat16)
    projected_entries = projected_entries.reshape(homolog_entries, residue_tally, HEADS, HEAD_CH)
    sigmoid_factor = jax.nn.sigmoid(jnp.dot(standardized_halfwidth, sigmoid_projection_matrix, preferred_element_type=jnp.float32))
    sigmoid_factor = sigmoid_factor.reshape(homolog_entries, residue_tally, FEATURE_WIDTH)
    pair_blocks = residue_couple_features.reshape(blocks, TOK_DEV, residue_tally, CZ)
    bias_f = logit_projection_matrix.astype(jnp.float32)

    def block_logits(block):
        normed, unused_scale = standardize_features(block.astype(jnp.float32))
        return jnp.einsum('ijc,ch->hij', normed.astype(jnp.bfloat16).astype(jnp.float32), bias_f)
    logits = lax.map(block_logits, pair_blocks)
    logits = logits.transpose(1, 0, 2, 3).reshape(HEADS, residue_tally, residue_tally)
    live = (residue_validity > 0)[None, None, :]
    masked = jnp.where(live, logits, -1000000000.0)
    row_top = lax.optimization_barrier(jnp.max(masked, axis=-1, keepdims=True))
    expo = jnp.where(live, jnp.exp(masked - row_top), 0.0)
    weights = expo / lax.optimization_barrier(jnp.sum(expo, axis=-1, keepdims=True))
    weights_low = weights.astype(jnp.bfloat16)
    blended_result = jnp.einsum('hij,sjhc->sihc', weights_low.astype(jnp.float32), projected_entries.astype(jnp.float32))
    blended_result = blended_result.reshape(homolog_entries, residue_tally, FEATURE_WIDTH)
    modulated_blend = sigmoid_factor * homolog_validity.astype(jnp.float32)[:, None, None]
    combined_heads = (modulated_blend * blended_result).astype(jnp.bfloat16)
    combined_heads_flattened = combined_heads.reshape(-1, FEATURE_WIDTH)
    module_result = jnp.dot(combined_heads_flattened, final_projection_matrix, preferred_element_type=jnp.float32).astype(jnp.bfloat16)
    module_result = module_result.reshape(homolog_entries, residue_tally * FEATURE_WIDTH)
    incoming_adjoint = result_adjoint.reshape(-1, FEATURE_WIDTH)
    blended_adjoint = jnp.dot(incoming_adjoint, final_projection_matrix.T, preferred_element_type=jnp.float32).reshape(homolog_entries, residue_tally, FEATURE_WIDTH)
    output_weight_gradient = jnp.dot(combined_heads_flattened.T, incoming_adjoint, preferred_element_type=jnp.float32)
    d_average = (blended_adjoint * modulated_blend).astype(jnp.bfloat16).reshape(homolog_entries, residue_tally, HEADS, HEAD_CH)
    sigmoid_factor_adjoint = (blended_adjoint * blended_result * modulated_blend * (1.0 - sigmoid_factor)).astype(jnp.bfloat16).reshape(-1, FEATURE_WIDTH)
    avg_blocks = d_average.reshape(N_SEQ, SEQ_DEV, residue_tally, HEADS, HEAD_CH).astype(jnp.float32)
    val_blocks = projected_entries.reshape(N_SEQ, SEQ_DEV, residue_tally, HEADS, HEAD_CH).astype(jnp.float32)

    def add_logit_grad(running, pieces):
        partial_sum = jnp.einsum('sihc,sjhc->hij', pieces[0], pieces[1])
        rounded = lax.optimization_barrier(partial_sum.astype(jnp.bfloat16))
        return (running + rounded.astype(jnp.float32), None)
    d_weights, unused_out = lax.scan(add_logit_grad, jnp.zeros((HEADS, residue_tally, residue_tally), jnp.float32), (avg_blocks, val_blocks))
    row_sum = lax.optimization_barrier(jnp.sum(weights * d_weights, axis=-1, keepdims=True))
    d_logits = (weights * (d_weights - row_sum)).astype(jnp.bfloat16)
    dlogit_blocks = d_logits.reshape(HEADS, blocks, TOK_DEV, residue_tally).transpose(1, 0, 2, 3)

    def block_back(pieces):
        block, dscore = pieces
        normed, scale = standardize_features(block.astype(jnp.float32))
        dscore_f = dscore.astype(jnp.float32)
        bias_part = jnp.einsum('ijc,hij->ch', normed.astype(jnp.bfloat16).astype(jnp.float32), dscore_f)
        standardized_adjoint = jnp.einsum('hij,ch->ijc', dscore_f, bias_f)
        return (standardize_backward(standardized_adjoint, normed, scale).astype(jnp.bfloat16), bias_part)
    pair_parts, bias_parts = lax.map(block_back, (pair_blocks, dlogit_blocks))
    pairwise_gradient = pair_parts.reshape(residue_tally, residue_tally, CZ)
    bias_weight_gradient = lax.optimization_barrier(jnp.sum(bias_parts, axis=0))
    weight_blocks = weights_low.reshape(HEADS, blocks, TOK_DEV, residue_tally).transpose(1, 0, 2, 3).astype(jnp.float32)
    davg_blocks = d_average.reshape(homolog_entries, blocks, TOK_DEV, HEADS, HEAD_CH).transpose(1, 0, 2, 3, 4)
    davg_blocks = davg_blocks.astype(jnp.float32)

    def add_value_grad(running, pieces):
        partial_sum = jnp.einsum('hij,sihc->sjhc', pieces[0], pieces[1])
        rounded = lax.optimization_barrier(partial_sum.astype(jnp.bfloat16))
        return (running + rounded.astype(jnp.float32), None)
    projected_entries_adjoint, unused_out = lax.scan(add_value_grad, jnp.zeros((homolog_entries, residue_tally, HEADS, HEAD_CH), jnp.float32), (weight_blocks, davg_blocks))
    projected_entries_adjoint_half = projected_entries_adjoint.astype(jnp.bfloat16).reshape(-1, FEATURE_WIDTH)
    standardized_adjoint = jnp.dot(projected_entries_adjoint_half, content_projection_matrix.T, preferred_element_type=jnp.float32)
    standardized_adjoint = standardized_adjoint + jnp.dot(sigmoid_factor_adjoint, sigmoid_projection_matrix.T, preferred_element_type=jnp.float32)
    value_weight_gradient = jnp.dot(standardized_halfwidth.T, projected_entries_adjoint_half, preferred_element_type=jnp.float32)
    gate_weight_gradient = jnp.dot(standardized_halfwidth.T, sigmoid_factor_adjoint, preferred_element_type=jnp.float32)
    homolog_feature_derivative = standardize_backward(standardized_adjoint.reshape(homolog_entries, residue_tally, FEATURE_WIDTH), homolog_standardized, homolog_standardize_factor)
    homolog_feature_derivative = homolog_feature_derivative.astype(jnp.bfloat16).reshape(homolog_entries, residue_tally * FEATURE_WIDTH)
    return (module_result, homolog_feature_derivative, pairwise_gradient, value_weight_gradient, gate_weight_gradient, bias_weight_gradient, output_weight_gradient)
```

```python
import functools
import jax
import jax.numpy as jnp
from jax import lax
from jax.experimental import pallas as pl
from jax.experimental.pallas import tpu as pltpu
from jax.sharding import Mesh, PartitionSpec as P

F32, BF = jnp.float32, jnp.bfloat16
HEADS, CH, CZ, SEQS, TOK, COLS = 8, 8, 128, 54, 128, 256
WIDTH = HEADS * CH
SC = SEQS * CH
ROWS = SEQS * TOK
HALF = ROWS // 2
STEP = 16
PAY = TOK + 16
EPS = 1e-05
SPAN = 6 * TOK
VMEM = 60 * 1024 * 1024

NT = (((1,), (1,)), ((), ()))
TN = (((0,), (0,)), ((), ()))
NN = (((1,), (0,)), ((), ()))


def dot(a, b, dims=NN):
    return lax.dot_general(a, b, dims, preferred_element_type=F32)


def split3(a):
    hi = a.astype(BF).astype(F32)
    rest = a - hi
    mid = rest.astype(BF).astype(F32)
    low = (rest - mid).astype(BF).astype(F32)
    return hi, mid, low


def group_mean(a, ones):
    hi = a.astype(BF)
    low = (a - hi.astype(F32)).astype(BF)
    return dot(hi, ones) + dot(low, ones)


def other_half(a):
    return jnp.concatenate([a[:, TOK:], a[:, :TOK]], axis=1)


def pair_forward_kernel(core_ref, live_ref, wl_ref, x_ref, e_ref, pay_ref, rows, tops, sums):
    g = pl.program_id(0)
    lane = lax.broadcasted_iota(jnp.int32, (HEADS, TOK), 1)

    @pl.when(g == 0)
    def _():
        tops[...] = jnp.zeros_like(tops)
        sums[...] = jnp.zeros_like(sums)

    @pl.when(g < TOK // STEP)
    def _():
        live = live_ref[...] > 0
        flip = core_ref[0] > 0
        wl = wl_ref[...]
        top_all, sum_all = tops[...], sums[...]
        for i in range(STEP):
            x = x_ref[i].astype(F32)
            center = x - jnp.mean(x, axis=-1, keepdims=True)
            scale = lax.rsqrt(jnp.mean(center * center, axis=-1, keepdims=True) + EPS)
            z = (center * scale).astype(BF)
            logits = dot(wl, z, NT)
            masked = jnp.where(live, logits, -1000000000.0)
            top = jnp.max(masked, axis=-1, keepdims=True)
            e = jnp.where(live, jnp.exp(masked - top), 0.0)
            total = jnp.sum(e, axis=-1, keepdims=True)
            e_ref[i] = e
            rows[:, i, :] = jnp.where(flip, other_half(e), e)
            here = lane == g * STEP + i
            top_all = jnp.where(here, top, top_all)
            sum_all = jnp.where(here, total, sum_all)
        tops[...] = top_all
        sums[...] = sum_all
        pay_ref[...] = rows[...].astype(BF)

    @pl.when(g == TOK // STEP)
    def _():
        rows[...] = jnp.zeros_like(rows)
        for k, part in enumerate(split3(tops[...]) + split3(sums[...])):
            rows[:, k, 0:TOK] = part
        pay_ref[...] = rows[...].astype(BF)


def pair_forward(core, live, wl, pair):
    steps = TOK // STEP
    return pl.pallas_call(
        pair_forward_kernel,
        grid=(steps + 1,),
        in_specs=[
            pl.BlockSpec(memory_space=pltpu.SMEM),
            pl.BlockSpec((1, COLS), lambda g: (0, 0)),
            pl.BlockSpec((HEADS, CZ), lambda g: (0, 0)),
            pl.BlockSpec((STEP, COLS, CZ), lambda g: (jnp.minimum(g, steps - 1), 0, 0)),
        ],
        out_specs=[
            pl.BlockSpec((STEP, HEADS, COLS), lambda g: (jnp.minimum(g, steps - 1), 0, 0)),
            pl.BlockSpec((HEADS, 16, COLS), lambda g: (0, g, 0)),
        ],
        out_shape=[
            jax.ShapeDtypeStruct((TOK, HEADS, COLS), F32),
            jax.ShapeDtypeStruct((HEADS, PAY, COLS), BF),
        ],
        scratch_shapes=[
            pltpu.VMEM((HEADS, STEP, COLS), F32),
            pltpu.VMEM((HEADS, TOK), F32),
            pltpu.VMEM((HEADS, TOK), F32),
        ],
        compiler_params=pltpu.CompilerParams(vmem_limit_bytes=VMEM),
        cost_estimate=pl.CostEstimate(flops=10**9, bytes_accessed=12 * 10**6, transcendentals=300000),
        name="pair_forward",
    )(core, live, wl, pair)


def pair_backward_kernel(core_ref, wl_ref, x_ref, e_ref, dw_ref, st_ref, out_ref, bias_ref, rows, stat):
    g = pl.program_id(0)
    lane = lax.broadcasted_iota(jnp.int32, (HEADS, TOK), 1)

    @pl.when(g == 0)
    def _():
        bias_ref[...] = jnp.zeros_like(bias_ref)

    flip = core_ref[0] > 0
    wl = wl_ref[...]
    stat[...] = st_ref[...].astype(F32)
    factor = stat[:, 0, 0:TOK] + stat[:, 1, 0:TOK] + stat[:, 2, 0:TOK]
    rows[...] = dw_ref[...].astype(F32)
    bias = bias_ref[...]
    for i in range(STEP):
        x = x_ref[i].astype(F32)
        center = x - jnp.mean(x, axis=-1, keepdims=True)
        scale = lax.rsqrt(jnp.mean(center * center, axis=-1, keepdims=True) + EPS)
        zhat = center * scale
        mine = jnp.sum(jnp.where(lane == g * STEP + i, factor, 0.0), axis=-1, keepdims=True)
        dw = rows[:, i, :]
        dw = jnp.where(flip, other_half(dw), dw)
        dlogits = (e_ref[i] * mine * dw).astype(BF)
        bias = bias + dot(dlogits, zhat.astype(BF))
        dz = dot(dlogits, wl, TN)
        first = jnp.mean(dz, axis=-1, keepdims=True)
        second = jnp.mean(dz * zhat, axis=-1, keepdims=True)
        out_ref[i] = (scale * (dz - first - zhat * second)).astype(BF)
    bias_ref[...] = bias


def pair_backward(core, wl, pair, e, dw):
    return pl.pallas_call(
        pair_backward_kernel,
        grid=(TOK // STEP,),
        in_specs=[
            pl.BlockSpec(memory_space=pltpu.SMEM),
            pl.BlockSpec((HEADS, CZ), lambda g: (0, 0)),
            pl.BlockSpec((STEP, COLS, CZ), lambda g: (g, 0, 0)),
            pl.BlockSpec((STEP, HEADS, COLS), lambda g: (g, 0, 0)),
            pl.BlockSpec((HEADS, STEP, COLS), lambda g: (0, g, 0)),
            pl.BlockSpec((HEADS, STEP, COLS), lambda g: (0, TOK // STEP, 0)),
        ],
        out_specs=[
            pl.BlockSpec((STEP, COLS, CZ), lambda g: (g, 0, 0)),
            pl.BlockSpec((HEADS, CZ), lambda g: (0, 0)),
        ],
        out_shape=[
            jax.ShapeDtypeStruct((TOK, COLS, CZ), BF),
            jax.ShapeDtypeStruct((HEADS, CZ), F32),
        ],
        scratch_shapes=[pltpu.VMEM((HEADS, STEP, COLS), F32), pltpu.VMEM((HEADS, STEP, COLS), F32)],
        compiler_params=pltpu.CompilerParams(vmem_limit_bytes=VMEM),
        cost_estimate=pl.CostEstimate(flops=10**9, bytes_accessed=20 * 10**6, transcendentals=30000),
        name="pair_backward",
    )(core, wl, pair, e, dw, dw)


def unpack_tokens(src_ref, wide, dst):
    for k in range(TOK // 2):
        wide[:, k, :] = src_ref[:, k * 128 : (k + 1) * 128].astype(F32)


def msa_forward_kernel(
    x_ref, ra_ref, ones_ref, wvt_ref, wgt_ref, wf_ref, live_ref,
    vd_ref, gate_ref, dmix_ref, mn_ref, rao_ref, xhat_ref, rstd_ref, wide, flat,
):
    ones = ones_ref[...]
    unpack_tokens(ra_ref, wide, None)
    packed = wide[...].reshape(HALF, 128)
    flat[pl.ds(0, HALF, stride=2), :] = packed[:, 0:WIDTH]
    flat[pl.ds(1, HALF, stride=2), :] = packed[:, WIDTH:]
    rao_ref[...] = flat[...].astype(BF)
    unpack_tokens(x_ref, wide, None)
    packed = wide[...].reshape(HALF, 128)
    center = packed - dot(packed.astype(BF), ones)
    rstd = lax.rsqrt(group_mean(center * center, ones) + EPS)
    xhat = center * rstd
    xhat_ref[...] = xhat
    rstd_ref[...] = rstd
    flat[pl.ds(0, HALF, stride=2), :] = xhat[:, 0:WIDTH]
    flat[pl.ds(1, HALF, stride=2), :] = xhat[:, WIDTH:]
    mn_ref[...] = flat[...].astype(BF)
    for n in range(ROWS // SPAN):
        at = slice(n * SPAN, (n + 1) * SPAN)
        mn = mn_ref[at, :]
        v = dot(wvt_ref[...], mn, NT)
        gate = jax.nn.sigmoid(dot(wgt_ref[...], mn, NT))
        dmix = dot(wf_ref[...], rao_ref[at, :], NT)
        da = dmix * (gate * live_ref[:, at])
        gate_ref[:, at] = gate
        dmix_ref[:, at] = dmix
        for h in range(HEADS):
            for s in range(0, SPAN // TOK, 2):
                row = n * (SPAN // TOK) * CH + s * CH
                for arr, base in ((v, 0), (da, SC)):
                    part = arr[h * CH : (h + 1) * CH, :]
                    two = jnp.concatenate(
                        [part[:, s * TOK : (s + 1) * TOK], part[:, (s + 1) * TOK : (s + 2) * TOK]], axis=0
                    )
                    vd_ref[h, base + row : base + row + 16, :] = two.astype(BF)


def msa_forward(x, ra, ones, wvt, wgt, wf, live):
    return pl.pallas_call(
        msa_forward_kernel,
        out_shape=[
            jax.ShapeDtypeStruct((HEADS, 2 * SC, TOK), BF),
            jax.ShapeDtypeStruct((WIDTH, ROWS), F32),
            jax.ShapeDtypeStruct((WIDTH, ROWS), F32),
            jax.ShapeDtypeStruct((ROWS, WIDTH), BF),
            jax.ShapeDtypeStruct((ROWS, WIDTH), BF),
            jax.ShapeDtypeStruct((HALF, 128), F32),
            jax.ShapeDtypeStruct((HALF, 128), F32),
        ],
        scratch_shapes=[pltpu.VMEM((SEQS, TOK // 2, 128), F32), pltpu.VMEM((ROWS, WIDTH), F32)],
        compiler_params=pltpu.CompilerParams(vmem_limit_bytes=VMEM),
        cost_estimate=pl.CostEstimate(flops=10**9, bytes_accessed=14 * 10**6, transcendentals=500000),
        name="msa_forward",
    )(x, ra, ones, wvt, wgt, wf, live)


def pack_tokens(flat, wide, dst_ref):
    pass


def msa_backward_kernel(
    od_ref, gate_ref, dmix_ref, live_ref, mn_ref, ra_ref, xhat_ref, rstd_ref, ones_ref, wvg_ref, wf_ref,
    res_ref, dx_ref, wg_ref, wide, flat, flat2,
):
    acc_in = jnp.zeros((2 * WIDTH, WIDTH), F32)
    acc_out = jnp.zeros((WIDTH, WIDTH), F32)
    for n in range(ROWS // SPAN):
        at = slice(n * SPAN, (n + 1) * SPAN)
        first = n * (SPAN // TOK) * CH
        heads_o, heads_v = [], []
        for h in range(HEADS):
            o = od_ref[h, first : first + 6 * CH, :].astype(F32)
            dv = od_ref[h, SC + first : SC + first + 6 * CH, :].astype(F32)
            heads_o.append(jnp.concatenate([o[s * CH : (s + 1) * CH] for s in range(6)], axis=1))
            heads_v.append(jnp.concatenate([dv[s * CH : (s + 1) * CH] for s in range(6)], axis=1))
        average = jnp.concatenate(heads_o, axis=0)
        dvalues = jnp.concatenate(heads_v, axis=0)
        gate = gate_ref[:, at]
        gated = gate * live_ref[:, at]
        mixed = (gated * average).astype(BF)
        dgate = dmix_ref[:, at] * average * gated * (1.0 - gate)
        both = jnp.concatenate([dvalues, dgate], axis=0).astype(BF)
        flat[at, :] = dot(mixed, wf_ref[...], TN)
        flat2[at, :] = dot(both, wvg_ref[...], TN)
        acc_in = acc_in + dot(both, mn_ref[at, :])
        acc_out = acc_out + dot(mixed, ra_ref[at, :])
    wg_ref[0 : 2 * WIDTH, :] = acc_in
    wg_ref[2 * WIDTH :, :] = acc_out
    res = jnp.concatenate([flat[pl.ds(0, HALF, stride=2), :], flat[pl.ds(1, HALF, stride=2), :]], axis=1)
    wide[...] = res.reshape(SEQS, TOK // 2, 128)
    for k in range(TOK // 2):
        res_ref[:, k * 128 : (k + 1) * 128] = wide[:, k, :].astype(BF)
    dm = jnp.concatenate([flat2[pl.ds(0, HALF, stride=2), :], flat2[pl.ds(1, HALF, stride=2), :]], axis=1)
    ones = ones_ref[...]
    xhat = xhat_ref[...]
    mean = group_mean(dm, ones)
    second = group_mean(dm * xhat, ones)
    dx = rstd_ref[...] * (dm - mean - xhat * second)
    wide[...] = dx.reshape(SEQS, TOK // 2, 128)
    for k in range(TOK // 2):
        dx_ref[:, k * 128 : (k + 1) * 128] = wide[:, k, :].astype(BF)


def msa_backward(od, gate, dmix, live, mn, ra, xhat, rstd, ones, wvg, wf):
    return pl.pallas_call(
        msa_backward_kernel,
        out_shape=[
            jax.ShapeDtypeStruct((SEQS, TOK * WIDTH), BF),
            jax.ShapeDtypeStruct((SEQS, TOK * WIDTH), BF),
            jax.ShapeDtypeStruct((3 * WIDTH, WIDTH), F32),
        ],
        scratch_shapes=[
            pltpu.VMEM((SEQS, TOK // 2, 128), F32),
            pltpu.VMEM((ROWS, WIDTH), F32),
            pltpu.VMEM((ROWS, WIDTH), F32),
        ],
        compiler_params=pltpu.CompilerParams(vmem_limit_bytes=VMEM),
        cost_estimate=pl.CostEstimate(flops=10**9, bytes_accessed=14 * 10**6, transcendentals=0),
        name="msa_backward",
    )(od, gate, dmix, live, mn, ra, xhat, rstd, ones, wvg, wf)


def head_forward_kernel(q_ref, va_ref, vo_ref, *refs):
    e_refs, (o_ref, scale_ref), dw_refs = refs[:8], refs[8:10], refs[10:18]
    vs, da, dat = refs[18:]
    q = q_ref[0]
    for m in range(8):
        at = jnp.bitwise_xor(q, m)
        vs[0:SC, m * COLS : m * COLS + TOK] = va_ref[at, 0:SC, :]
        vs[0:SC, m * COLS + TOK : (m + 1) * COLS] = vo_ref[at]
    vs[SC:, :] = jnp.ones((16, 8 * COLS), BF)
    for b in range(8):
        parts = [e_refs[m][b, TOK : TOK + 16, 0:TOK].astype(F32) for m in range(8)]
        top = jnp.concatenate([p[0:1] + p[1:2] + p[2:3] for p in parts], axis=0)
        total = jnp.concatenate([p[3:4] + p[4:5] + p[5:6] for p in parts], axis=0)
        rel = jnp.exp(top - jnp.max(top, axis=0, keepdims=True))
        scale_ref[b] = rel / jnp.sum(rel * total, axis=0, keepdims=True)
        da[0:SC, b * TOK : (b + 1) * TOK] = va_ref[b, SC : 2 * SC, :]
    for p in range(4):
        acc = jnp.zeros((SC, 2 * TOK), F32)
        for m in range(8):
            e = jnp.concatenate([e_refs[m][2 * p, 0:TOK, :], e_refs[m][2 * p + 1, 0:TOK, :]], axis=0)
            factor = jnp.concatenate([scale_ref[2 * p, m : m + 1, :], scale_ref[2 * p + 1, m : m + 1, :]], axis=1)
            acc = acc + factor * dot(vs[0:SC, m * COLS : (m + 1) * COLS], e, NT)
        o_ref[2 * p] = acc[:, :TOK].astype(BF)
        o_ref[2 * p + 1] = acc[:, TOK:].astype(BF)
        cols = slice(2 * p * TOK, (2 * p + 2) * TOK)
        row = -jnp.sum(da[0:SC, cols].astype(F32) * acc, axis=0, keepdims=True)
        extra = jnp.concatenate(list(split3(row)) + [jnp.zeros((13, 2 * TOK), F32)], axis=0)
        da[SC:, cols] = extra.astype(BF)
        dat[cols, :] = da[:, cols].T
    for m in range(8):
        dw = dot(dat[...], vs[:, m * COLS : (m + 1) * COLS])
        dw_refs[m][...] = dw.astype(BF).reshape(8, TOK, COLS)


def head_forward(q, va, vo, es):
    return pl.pallas_call(
        head_forward_kernel,
        in_specs=[pl.BlockSpec(memory_space=pltpu.SMEM)] + [pl.BlockSpec(memory_space=pltpu.VMEM)] * 10,
        out_shape=[
            jax.ShapeDtypeStruct((8, SC, TOK), BF),
            jax.ShapeDtypeStruct((8, 8, TOK), F32),
        ]
        + [jax.ShapeDtypeStruct((8, TOK, COLS), BF)] * 8,
        scratch_shapes=[
            pltpu.VMEM((SC + 16, 8 * COLS), BF),
            pltpu.VMEM((SC + 16, 8 * TOK), BF),
            pltpu.VMEM((8 * TOK, SC + 16), BF),
        ],
        compiler_params=pltpu.CompilerParams(vmem_limit_bytes=VMEM),
        cost_estimate=pl.CostEstimate(flops=4 * 10**9, bytes_accessed=14 * 10**6, transcendentals=0),
        name="head_forward",
    )(q, va, vo, *es)


def head_backward_kernel(q_ref, va_ref, scale_ref, *refs):
    e_refs, (own_ref, oth_ref) = refs[:8], refs[8:]
    q = q_ref[0]
    for m in range(8):
        at = jnp.bitwise_xor(q, m)
        da = jnp.concatenate(
            [(va_ref[b, SC : 2 * SC, :].astype(F32) * scale_ref[b, m : m + 1, :]).astype(BF) for b in range(8)], axis=1
        )
        e = jnp.concatenate([e_refs[m][b, 0:TOK, :] for b in range(8)], axis=0)
        dv = dot(da, e).astype(BF)
        own_ref[at] = dv[:, :TOK]
        oth_ref[at] = dv[:, TOK:]


def head_backward(q, va, scale, es):
    return pl.pallas_call(
        head_backward_kernel,
        in_specs=[pl.BlockSpec(memory_space=pltpu.SMEM)] + [pl.BlockSpec(memory_space=pltpu.VMEM)] * 10,
        out_shape=[jax.ShapeDtypeStruct((8, SC, TOK), BF)] * 2,
        compiler_params=pltpu.CompilerParams(vmem_limit_bytes=VMEM),
        cost_estimate=pl.CostEstimate(flops=2 * 10**9, bytes_accessed=8 * 10**6, transcendentals=0),
        name="head_backward",
    )(q, va, scale, *es)


def sum_weights_kernel(scale_ref, *refs):
    out_ref = refs[8]
    for b in range(8):
        total = refs[0][b].astype(F32)
        for m in range(1, 8):
            total = total + refs[m][b].astype(F32)
        out_ref[b, 0:TOK, :] = total.astype(BF)
        stats = jnp.concatenate(list(split3(scale_ref[b, 0:1, :])) + [jnp.zeros((13, TOK), F32)], axis=0)
        out_ref[b, TOK : TOK + 16, 0:TOK] = stats.astype(BF)
        out_ref[b, TOK : TOK + 16, TOK:] = jnp.zeros((16, TOK), BF)


def sum_weights(scale, parts):
    return pl.pallas_call(
        sum_weights_kernel,
        out_shape=jax.ShapeDtypeStruct((8, PAY, COLS), BF),
        compiler_params=pltpu.CompilerParams(vmem_limit_bytes=VMEM),
        cost_estimate=pl.CostEstimate(flops=10**7, bytes_accessed=5 * 10**6, transcendentals=0),
        name="sum_weights",
    )(scale, *parts)


PAIRS = ("yl", "z")
GROUP = ("yh", "x")
SIZES = {"yh": 2, "x": 4, "core": 2, "yl": 2, "z": 4}


def swap(a, axes, mask):
    size = 1
    for axis in axes:
        size *= SIZES[axis]
    return lax.ppermute(a, axes, [(n, n ^ mask) for n in range(size)])


def total_over_all(a):
    for axis, masks in (("core", (1,)), ("x", (1, 2)), ("z", (1, 2)), ("yl", (1,)), ("yh", (1,))):
        for mask in masks:
            a = a + swap(a, (axis,), mask)
    return a


def exchange(a):
    return lax.all_to_all(a, GROUP, 0, 0, tiled=True)


def per_device(msa, pair, token_live, seq_live, wv, wg, wl, wf, adjoint):
    q = lax.axis_index(PAIRS).astype(jnp.int32)
    core = lax.axis_index("core").astype(jnp.int32)
    live = lax.dynamic_slice_in_dim(token_live, q * COLS, COLS, 0).reshape(1, COLS)
    seq_row = jnp.repeat(seq_live.astype(F32), TOK).reshape(1, ROWS)
    block = jnp.arange(128) // WIDTH
    ones = jnp.where(block[:, None] == block[None, :], 1.0 / WIDTH, 0.0).astype(BF)
    q, core = q.reshape(1), core.reshape(1)

    wlt = wl.T
    e, pay = pair_forward(core, live, wlt, pair)
    pay = exchange(pay)
    es = [pay] + [swap(pay, PAIRS, m) for m in range(1, 8)]

    msa, pay0 = lax.optimization_barrier((msa, pay))
    vd, gate, dmix, mn, ra, xhat, rstd = msa_forward(msa, adjoint, ones, wv.T, wg.T, wf, seq_row)
    va = exchange(vd)
    vo = swap(va[:, :SC, :], ("core",), 1)

    o, scale, *dws = head_forward(q, va, vo, es)
    parts = [dws[0]] + [swap(dws[m], PAIRS, m) for m in range(1, 8)]
    own, oth = head_backward(q, va, scale, es)
    dv = (own.astype(F32) + swap(oth, ("core",), 1).astype(F32)).astype(BF)
    od = exchange(jnp.concatenate([o, dv], axis=1))
    result, dmsa, grads = msa_backward(
        od, gate, dmix, seq_row, mn, ra, xhat, rstd, ones, jnp.concatenate([wv.T, wg.T], axis=0), wf
    )
    grads = total_over_all(grads.reshape(3 * WIDTH // 2, 2 * WIDTH)).reshape(3, WIDTH, WIDTH)

    dw = exchange(sum_weights(scale, parts))
    dpair, bias = pair_backward(core, wlt, pair, e, dw)
    bias = total_over_all(bias)
    return result, dmsa, dpair, grads[0].T, grads[1].T, bias.T, grads[2]


def solution(mesh):
    names = tuple(SIZES)
    fine = Mesh(mesh.devices.reshape(tuple(SIZES.values())), names)
    axial, seq = ("yh", "x", "core"), ("yl", "z")
    placed = (P(seq, axial), P(axial, seq, None), P(), P(seq), P(), P(), P(), P(), P(seq, axial))
    return jax.shard_map(
        per_device,
        mesh=fine,
        in_specs=placed,
        out_specs=(P(seq, axial), P(seq, axial), P(axial, seq, None), P(), P(), P(), P()),
        check_vma=False,
    )
```
